256 devices in a mesh: row: 16 (over y_hi, x, core), col: 16 (over z, y_lo).
Axes of the slice: x: 4, y: 4 (y_hi: 2, y_lo: 2; y = y_hi * 2 + y_lo), z: 8, core: 2. Of those that a mesh axis runs over, the one named last changes fastest.
Arguments:
- integrals: bfloat16 [896, 32, 28672], P('row', 'col'), may hold values from -0.0068359375 to 0.0068359375
- amplitudes: bfloat16 [896, 917504], P('row', 'col'), may hold values from -6 to 6
Outputs:
- ladder_out: bfloat16 [32, 32, 32, 32], P('col', None, 'row')
The draws below stay inside these ranges and needn't reach their ends.
All inputs are finite; a program needn't handle non-finite values.
Results may differ from the reference program's by a relative error of at most 0.0051.
Values may be sent and summed in bfloat16 or wider, within the bound.
A program may use at most 320 MiB of HBM per device.

```python
import jax
import jax.numpy as jnp
from jax import lax

NV = 896
VB = 32
OB = 32
PAIRS = 1024


def shard_levels(key, dims, cuts, least, top_value):
    def one(dim, shards_of):
        steps = jax.random.uniform(jax.random.fold_in(jax.random.fold_in(key, 6), dim), (shards_of,), jnp.float32, least / len(cuts), top_value / len(cuts))
        return jnp.repeat(jnp.exp(steps), dims[dim] // shards_of).reshape((-1,) + (1,) * (len(dims) - dim - 1))

    gain = one(*cuts[0])
    for cut in cuts[1:]:
        gain = gain * one(*cut)
    return gain


def gaussian(stream_key, dims, deviation, limit, split=(), kind=jnp.bfloat16):
    entries = deviation * jax.random.normal(stream_key, dims, jnp.float32)
    if split:
        entries = entries * shard_levels(stream_key, dims, split, -0.22, 0.18)
    return jnp.clip(entries, -limit, limit).astype(kind)


def setup_inputs(seed: int = 0) -> dict:
    keys = jax.random.split(jax.random.key(seed), 3)
    integrals = gaussian(keys[0], (NV, VB, NV * VB), (NV * NV) ** -0.5, 0.0068359375, ((0, 16), (1, 16)))
    amplitudes = gaussian(keys[1], (NV, NV * PAIRS), 1.0, 6.0, ((0, 16), (1, 16)))
    return dict(integrals=integrals, amplitudes=amplitudes)


def reference(integrals, amplitudes):
    weights = integrals.reshape(NV, VB, NV, VB)
    amp_rows = amplitudes.reshape(NV, NV, OB * OB)

    def advance(running, orbital):
        weight_slab = lax.dynamic_index_in_dim(weights, orbital, 0, keepdims=False)
        amp_slab = lax.dynamic_index_in_dim(amp_rows, orbital, 0, keepdims=False)
        flattened = jnp.transpose(weight_slab, (0, 2, 1)).reshape(VB * VB, NV)
        return running + jnp.dot(flattened, amp_slab, preferred_element_type=jnp.float32), None

    starting = jnp.zeros((VB * VB, OB * OB), jnp.float32)
    running, _ = lax.scan(advance, starting, jnp.arange(NV, dtype=jnp.int32))
    ladder = lax.optimization_barrier(running.astype(jnp.bfloat16)).reshape(VB, VB, OB, OB)
    mirror = jnp.transpose(ladder, (1, 0, 3, 2))
    return (ladder.astype(jnp.float32) + mirror.astype(jnp.float32)).astype(jnp.bfloat16)
```

```python
import jax
import jax.numpy as jnp
from jax import lax
from jax.experimental import pallas as pl
from jax.experimental.pallas import tpu as pltpu
from jax.sharding import PartitionSpec as P

MESH = pl.DeviceIdType.MESH
F32 = jnp.float32
BF16 = jnp.bfloat16

ROWS = 16
COLS = 16
CW = 56
DW = 56
VB = 32
OB = 32
PAIRS = OB * OB
GROUPS = 8
PIECES = 7
LANES = DW * VB // PIECES
TILES = LANES // 128
KP = TILES * 256


def kernel(w_ref, t_ref, o_ref, wbuf, tbuf, lhs, rhs, acc, folded, row_out, row_in, direct, mirror,
           col_out, col_in, w_send, w_recv, t_sem, row_send, row_recv, col_send, col_recv):
    r = lax.axis_index("row")
    q = lax.axis_index("col")
    z, y = q // 2, q % 2

    def step(g, h):
        far = (g // 2 + 3) // 4
        dz = (1 - far) * 4 * (g % 2) + far * (4 - g // 2) * (1 - 2 * h)
        dy = (1 - far) * h + far * (g % 2)
        return dz, dy

    def target(g, h):
        dz, dy = step(g, h)
        return lax.rem(z + dz + 8, 8) * 2 + lax.rem(y + dy, 2)

    def origin(g, h):
        dz, dy = step(g, h)
        return lax.rem(z - dz + 8, 8) * 2 + lax.rem(y - dy + 2, 2)

    def piece(g, h, k):
        return wbuf.at[g * 2 + h, :, :, pl.ds(pl.multiple_of(k * LANES, 128), LANES)]

    def send_piece(g, h, k):
        p = target(g, h)
        columns = pl.ds(pl.multiple_of(p * (DW * VB) + k * LANES, 128), LANES)
        return pltpu.make_async_remote_copy(
            src_ref=w_ref.at[:, :, columns], dst_ref=piece(g, h, k),
            send_sem=w_send.at[g, h], recv_sem=w_recv.at[g, h, k],
            device_id=(r, p), device_id_type=MESH)

    def local_copy(k):
        columns = pl.ds(pl.multiple_of(q * (DW * VB) + k * LANES, 128), LANES)
        return pltpu.make_async_copy(w_ref.at[:, :, columns], piece(0, 0, k), w_recv.at[0, 0, k])

    t_copy = pltpu.make_async_copy(t_ref, tbuf, t_sem)
    t_copy.start()

    barrier = pltpu.get_barrier_semaphore()
    for k in range(1, COLS):
        pl.semaphore_signal(barrier, inc=1, device_id=(r, lax.rem(q + k, COLS)), device_id_type=MESH)
    for k in range(1, ROWS):
        pl.semaphore_signal(barrier, inc=1, device_id=(lax.rem(r + k, ROWS), q), device_id_type=MESH)
    pl.semaphore_wait(barrier, COLS + ROWS - 2)

    @pl.loop(0, PIECES)
    def _(k):
        local_copy(k).start()
        send_piece(0, 1, k).start()

    @pl.loop(1, GROUPS)
    def _(g):
        @pl.loop(0, PIECES)
        def _(k):
            send_piece(g, 0, k).start()
            send_piece(g, 1, k).start()

    t_copy.wait()
    gap = jnp.zeros((8, PAIRS), F32)

    @pl.loop(0, PIECES)
    def _(k):
        for n in range(KP // 128):
            base = pl.multiple_of((k * (KP // 128) + n) * 2 * PAIRS, 128)
            first = tbuf[:, pl.ds(base, PAIRS)].astype(F32)
            second = tbuf[:, pl.ds(base + PAIRS, PAIRS)].astype(F32)
            both = jnp.concatenate([first, gap, second, gap], axis=0)
            lhs[k, :, n * 128:(n + 1) * 128] = both.T.astype(BF16)

    lane = lax.broadcasted_iota(jnp.int32, (64, 128), 1)
    pad = jnp.zeros((8, 128), F32)

    def compute(g):
        acc[...] = jnp.zeros_like(acc)

        @pl.loop(0, PIECES)
        def _(k):
            for h in range(2):
                pltpu.make_async_copy(piece(g, h, k), piece(g, h, k), w_recv.at[g, h, k]).wait()
            for h in range(2):
                for t in range(TILES):
                    columns = pl.ds(pl.multiple_of(k * LANES + t * 128, 128), 128)
                    x = wbuf[g * 2 + h, :, :, columns].astype(F32)
                    for a in range(2):
                        xa = jnp.concatenate([x[:, a, :], pad], axis=0)
                        for d in range(4):
                            rhs[t * 256 + d * 64:t * 256 + (d + 1) * 64,
                                h * 256 + a * 128:h * 256 + (a + 1) * 128] = (
                                jnp.where(lane // 32 == d, xa, 0.0).astype(BF16))
            acc[...] += jnp.dot(lhs[k], rhs[...], preferred_element_type=F32)

    low = lax.broadcasted_iota(jnp.int32, (32, 128), 1) < 64
    even = lane // 32 % 2 == 0

    def fold(x):
        x = x + pltpu.roll(x, 64, 1)
        return x + pltpu.roll(x, 32, 1)

    def scatter(g):
        for h in range(2):
            @pl.loop(0, ROWS)
            def _(p):
                rows = pl.ds(pl.multiple_of(p * 64, 64), 64)
                x = jnp.where(even, fold(acc[rows, h * 256:h * 256 + 128]),
                              fold(acc[rows, h * 256 + 128:h * 256 + 256]))
                folded[rows, :] = x
                row_out[g, p, h, 0] = jnp.where(low, x[:32], x[32:]).astype(BF16)

            @pl.loop(0, ROWS)
            def _(p):
                x0 = folded[pl.ds(2 * p, 32, stride=32), :]
                x1 = folded[pl.ds(2 * p + 1, 32, stride=32), :]
                row_out[g, p, h, 1] = jnp.where(low, x0, x1).astype(BF16)

        @pl.loop(1, ROWS)
        def _(k):
            p = lax.rem(r + k, ROWS)
            pltpu.make_async_remote_copy(
                src_ref=row_out.at[g, p], dst_ref=row_in.at[g, k - 1],
                send_sem=row_send.at[g], recv_sem=row_recv.at[g],
                device_id=(p, q), device_id_type=MESH).start()

    quarter = lax.broadcasted_iota(jnp.int32, (32, 128), 1) // 32

    def collect(g):
        pltpu.make_async_copy(row_in.at[g], row_in.at[g], row_recv.at[g]).wait()
        sums = [row_out[g, r, h, m].astype(F32) for h in range(2) for m in range(2)]
        for k in range(ROWS - 1):
            for h in range(2):
                for m in range(2):
                    sums[h * 2 + m] += row_in[g, k, h, m].astype(F32)
        turned = jnp.concatenate(sums, axis=0).T
        for h in range(2):
            p = origin(g, h)
            out = jnp.zeros((32, 128), F32)
            for n in range(4):
                block = turned[n * 32:(n + 1) * 32]
                shift = (n * 32 - h * 64) % 128
                moved = pltpu.roll(block, shift, 1) if shift else block
                out = jnp.where(quarter == n, moved, out)
                rows = pl.ds(pl.multiple_of((2 * p + n % 2) * 32, 32), 32)
                mirror[n // 2, rows, :] = pltpu.roll(block, (128 - h * 64 - 32) % 128, 1)
            direct[p] = out

    @pl.loop(0, GROUPS)
    def _(g):
        compute(g)
        scatter(g)

        @pl.when(g > 0)
        def _():
            collect(g - 1)

    collect(GROUPS - 1)

    def finish(p):
        out = jnp.zeros((32, 128), F32)
        for n in range(4):
            x = mirror[n // 2, pl.ds(2 * p + n % 2, 32, stride=32), :]
            out = jnp.where(quarter == n, pltpu.roll(x, n * 32, 1) if n else x, out)
        return direct[p] + out

    @pl.loop(1, COLS)
    def _(k):
        p = lax.rem(q + k, COLS)
        col_out[k - 1] = finish(p).astype(BF16)
        pltpu.make_async_remote_copy(
            src_ref=col_out.at[k - 1], dst_ref=col_in.at[k - 1],
            send_sem=col_send, recv_sem=col_recv,
            device_id=(r, p), device_id_type=MESH).start()

    total = finish(q)
    pltpu.make_async_copy(col_in, col_in, col_recv).wait()
    for k in range(COLS - 1):
        total += col_in[k].astype(F32)
    o_ref[...] = total.astype(BF16)

    pltpu.make_async_copy(col_out, col_out, col_send).wait()

    @pl.loop(0, GROUPS)
    def _(g):
        pltpu.make_async_copy(row_in.at[g], row_in.at[g], row_send.at[g]).wait()
        pltpu.make_async_copy(wbuf.at[g * 2 + 1], wbuf.at[g * 2 + 1], w_send.at[g, 1]).wait()

    @pl.loop(1, GROUPS)
    def _(g):
        pltpu.make_async_copy(wbuf.at[g * 2], wbuf.at[g * 2], w_send.at[g, 0]).wait()


def shards(integrals, amplitudes):
    out = pl.pallas_call(
        kernel,
        out_shape=jax.ShapeDtypeStruct((VB, 128), BF16),
        in_specs=[pl.BlockSpec(memory_space=pl.ANY)] * 2,
        out_specs=pl.BlockSpec(memory_space=pltpu.VMEM),
        scratch_shapes=[
            pltpu.VMEM((2 * GROUPS, CW, 2, DW * VB), BF16),
            pltpu.VMEM((CW, DW * PAIRS), BF16),
            pltpu.VMEM((PIECES, PAIRS, KP), BF16),
            pltpu.VMEM((KP, 512), BF16),
            pltpu.VMEM((PAIRS, 512), F32),
            pltpu.VMEM((PAIRS, 128), F32),
            pltpu.VMEM((GROUPS, ROWS, 2, 2, 32, 128), BF16),
            pltpu.VMEM((GROUPS, ROWS - 1, 2, 2, 32, 128), BF16),
            pltpu.VMEM((COLS, 32, 128), F32),
            pltpu.VMEM((2, PAIRS, 128), F32),
            pltpu.VMEM((COLS - 1, 32, 128), BF16),
            pltpu.VMEM((COLS - 1, 32, 128), BF16),
            pltpu.SemaphoreType.DMA((GROUPS, 2)),
            pltpu.SemaphoreType.DMA((GROUPS, 2, PIECES)),
            pltpu.SemaphoreType.DMA,
            pltpu.SemaphoreType.DMA((GROUPS,)),
            pltpu.SemaphoreType.DMA((GROUPS,)),
            pltpu.SemaphoreType.DMA,
            pltpu.SemaphoreType.DMA,
        ],
        compiler_params=pltpu.CompilerParams(
            collective_id=0, has_side_effects=True, vmem_limit_bytes=56 * 2**20),
        cost_estimate=pl.CostEstimate(flops=26 * 10**9, bytes_accessed=13 * 10**6, transcendentals=0),
    )(integrals, amplitudes)
    return jnp.transpose(out.reshape(VB, 2, 2, OB), (2, 0, 1, 3))


def solution(mesh):
    return jax.shard_map(
        shards,
        mesh=mesh,
        in_specs=(P("row", "col", None), P("row", "col")),
        out_specs=P("col", None, "row", None),
        check_vma=False,
    )
```

```python
import jax
import jax.numpy as jnp
from jax import lax
from jax.experimental import pallas as pl
from jax.experimental.pallas import tpu as pltpu
from jax.sharding import PartitionSpec as P

MESH = pl.DeviceIdType.MESH
F32 = jnp.float32
BF16 = jnp.bfloat16

ROWS = 16
CHIPS = 8
COLS = 16
CW = 56
DW = 56
VB = 32
OB = 32
PAIRS = OB * OB
GROUPS = 8
PIECES = 7
LANES = DW * VB // PIECES
TILES = LANES // 128
KP = TILES * 256


def kernel(w_ref, t_ref, o_ref, wbuf, tbuf, lhs, rhs, acc, cross, core_in, row_out, row_in, direct, mirror,
           col_out, col_in, w_send, w_recv, t_sem, core_send, core_recv, row_send, row_recv, col_send, col_recv):
    r = lax.axis_index("row")
    q = lax.axis_index("col")
    z, y = q // 2, q % 2
    u, c = r // 2, r % 2

    def step(g, h):
        i = g % 4
        far = (i + 3) // 4
        dz = (1 - far) * 4 * (1 - h) + far * (4 - i) * (1 - 2 * h)
        return dz, 1 - g // 4

    def target(g, h):
        dz, dy = step(g, h)
        return lax.rem(z + dz + 8, 8) * 2 + lax.rem(y + dy, 2)

    def origin(g, h):
        dz, dy = step(g, h)
        return lax.rem(z - dz + 8, 8) * 2 + lax.rem(y - dy + 2, 2)

    def piece(g, h, k):
        return wbuf.at[g * 2 + h, :, :, pl.ds(pl.multiple_of(k * LANES, 128), LANES)]

    def send_piece(g, h, k):
        p = target(g, h)
        columns = pl.ds(pl.multiple_of(p * (DW * VB) + k * LANES, 128), LANES)
        return pltpu.make_async_remote_copy(
            src_ref=w_ref.at[:, :, columns], dst_ref=piece(g, h, k),
            send_sem=w_send.at[g, h], recv_sem=w_recv.at[g, h, k],
            device_id=(r, p), device_id_type=MESH)

    def local_copy(k):
        columns = pl.ds(pl.multiple_of(q * (DW * VB) + k * LANES, 128), LANES)
        return pltpu.make_async_copy(w_ref.at[:, :, columns], piece(4, 1, k), w_recv.at[4, 1, k])

    t_copy = pltpu.make_async_copy(t_ref, tbuf, t_sem)
    t_copy.start()

    barrier = pltpu.get_barrier_semaphore()
    for k in range(1, COLS):
        pl.semaphore_signal(barrier, inc=1, device_id=(r, lax.rem(q + k, COLS)), device_id_type=MESH)
    for k in range(1, ROWS):
        pl.semaphore_signal(barrier, inc=1, device_id=(lax.rem(r + k, ROWS), q), device_id_type=MESH)
    pl.semaphore_wait(barrier, COLS + ROWS - 2)

    for slot in range(2 * GROUPS + PIECES - 2):
        @pl.loop(max(0, slot - PIECES + 2) // 2, min(GROUPS - 1, slot // 2) + 1)
        def _(g):
            send_piece(g, 0, slot - 2 * g).start()

            @pl.when(g != 4)
            def _():
                send_piece(g, 1, slot - 2 * g).start()

    @pl.loop(0, PIECES)
    def _(k):
        local_copy(k).start()

    t_copy.wait()
    gap = jnp.zeros((8, PAIRS), F32)

    @pl.loop(0, PIECES)
    def _(k):
        for n in range(KP // 128):
            base = pl.multiple_of((k * (KP // 128) + n) * 2 * PAIRS, 128)
            first = tbuf[:, pl.ds(base, PAIRS)].astype(F32)
            second = tbuf[:, pl.ds(base + PAIRS, PAIRS)].astype(F32)
            both = jnp.concatenate([first, gap, second, gap], axis=0)
            lhs[k, :, n * 128:(n + 1) * 128] = both.T.astype(BF16)

    @pl.loop(0, GROUPS)
    def _(g):
        acc[g] = jnp.zeros((PAIRS, 128), F32)

    quarter = lax.broadcasted_iota(jnp.int32, (CW, 128), 1) // 32
    pad = jnp.zeros((8, 128), F32)

    def compute(g, k):
        for h in range(2):
            pltpu.make_async_copy(piece(g, h, k), piece(g, h, k), w_recv.at[g, h, k]).wait()
        for t in range(TILES):
            columns = pl.ds(pl.multiple_of(k * LANES + t * 128, 128), 128)
            x = [wbuf[g * 2 + h, :, :, columns].astype(F32) for h in range(2)]
            x = [x[h][:, a, :] for h in range(2) for a in range(2)]
            for d in range(4):
                out = None
                for n in range(4):
                    moved = pltpu.roll(x[n], (n - d) % 4 * 32, 1) if n != d else x[n]
                    out = jnp.where(quarter == n, moved, out) if n else moved
                rhs[t * 256 + d * 64:t * 256 + (d + 1) * 64] = (
                    jnp.concatenate([out, pad], axis=0).astype(BF16))
        acc[g] += jnp.dot(lhs[k], rhs[...], preferred_element_type=F32)

    def cross_copy(g):
        return pltpu.make_async_remote_copy(
            src_ref=cross.at[g, 1 - c], dst_ref=core_in.at[g, 1],
            send_sem=core_send.at[g, 1], recv_sem=core_recv.at[g, 1],
            device_id=(r + 1 - 2 * c, q), device_id_type=MESH)

    def mine(p, core):
        return pl.ds(pl.multiple_of((p * 2 + core) * 64, 64), 64)

    def scatter(g):
        @pl.loop(0, CHIPS)
        def _(p):
            pltpu.make_async_remote_copy(
                src_ref=acc.at[g, mine(p, 1 - c)], dst_ref=core_in.at[g, 0, p],
                send_sem=core_send.at[g, 0], recv_sem=core_recv.at[g, 0],
                device_id=(r + 1 - 2 * c, q), device_id_type=MESH).start()

        for j in range(OB):
            cross[g, j // 2 % 2, j // 4, j % 2 * 32:(j % 2 + 1) * 32] = acc[g, pl.ds(j, 32, stride=32), :]
        cross_copy(g).start()

    def pair(g):
        pltpu.make_async_copy(core_in.at[g, 0], core_in.at[g, 0], core_recv.at[g, 0]).wait()
        cross_copy(g).wait_recv()

        @pl.loop(1, CHIPS)
        def _(k):
            p = lax.rem(u + k, CHIPS)
            row_out[g, p, 0] = (acc[g, mine(p, c)] + core_in[g, 0, p]).astype(BF16)
            row_out[g, p, 1] = (cross[g, c, p] + core_in[g, 1, p]).astype(BF16)
            pltpu.make_async_remote_copy(
                src_ref=row_out.at[g, p], dst_ref=row_in.at[g, k - 1],
                send_sem=row_send.at[g], recv_sem=row_recv.at[g],
                device_id=(p * 2 + c, q), device_id_type=MESH).start()

    low = lax.broadcasted_iota(jnp.int32, (32, 128), 1) < 64

    def collect(g):
        straight = acc[g, mine(u, c)] + core_in[g, 0, u]
        crossed = cross[g, c, u] + core_in[g, 1, u]
        pltpu.make_async_copy(row_in.at[g], row_in.at[g], row_recv.at[g]).wait()
        for k in range(CHIPS - 1):
            straight += row_in[g, k, 0].astype(F32)
            crossed += row_in[g, k, 1].astype(F32)
        turned = jnp.concatenate([straight, crossed], axis=0).T
        for h in range(2):
            p = origin(g, h)
            x0 = turned[h * 64:h * 64 + 32]
            x1 = turned[h * 64 + 32:h * 64 + 64]
            direct[p] = jnp.where(low, x0, pltpu.roll(x1, 64, 1))
            mirror[pl.ds(pl.multiple_of(p * 64, 64), 64), :] = turned[h * 64:h * 64 + 64]

    @pl.loop(0, GROUPS)
    def _(g):
        @pl.loop(0, PIECES)
        def _(k):
            compute(g, k)

            @pl.when((k == 1) & (g > 0))
            def _():
                pair(g - 1)

            @pl.when((k == 4) & (g > 0))
            def _():
                collect(g - 1)

        scatter(g)

    pair(GROUPS - 1)
    collect(GROUPS - 1)

    def finish(p):
        x0 = mirror[pl.ds(2 * p, 32, stride=32), :]
        x1 = mirror[pl.ds(2 * p + 1, 32, stride=32), :]
        return direct[p] + jnp.where(low, pltpu.roll(x0, 64, 1), x1)

    @pl.loop(1, COLS, unroll=5)
    def _(k):
        p = lax.rem(q + k, COLS)
        col_out[k - 1] = finish(p).astype(BF16)
        pltpu.make_async_remote_copy(
            src_ref=col_out.at[k - 1], dst_ref=col_in.at[k - 1],
            send_sem=col_send, recv_sem=col_recv,
            device_id=(r, p), device_id_type=MESH).start()

    total = finish(q)
    pltpu.make_async_copy(col_in, col_in, col_recv).wait()
    for k in range(COLS - 1):
        total += col_in[k].astype(F32)
    o_ref[...] = total.astype(BF16)

    pltpu.make_async_copy(col_out, col_out, col_send).wait()

    @pl.loop(0, GROUPS)
    def _(g):
        pltpu.make_async_copy(core_in.at[g, 0], core_in.at[g, 0], core_send.at[g, 0]).wait()
        cross_copy(g).wait_send()
        pltpu.make_async_copy(row_in.at[g], row_in.at[g], row_send.at[g]).wait()
        pltpu.make_async_copy(wbuf.at[g * 2], wbuf.at[g * 2], w_send.at[g, 0]).wait()

        @pl.when(g != 4)
        def _():
            pltpu.make_async_copy(wbuf.at[g * 2 + 1], wbuf.at[g * 2 + 1], w_send.at[g, 1]).wait()


def shards(integrals, amplitudes):
    out = pl.pallas_call(
        kernel,
        out_shape=jax.ShapeDtypeStruct((VB, 128), BF16),
        in_specs=[pl.BlockSpec(memory_space=pl.ANY)] * 2,
        out_specs=pl.BlockSpec(memory_space=pltpu.VMEM),
        scratch_shapes=[
            pltpu.VMEM((2 * GROUPS, CW, 2, DW * VB), BF16),
            pltpu.VMEM((CW, DW * PAIRS), BF16),
            pltpu.VMEM((PIECES, PAIRS, KP), BF16),
            pltpu.VMEM((KP, 128), BF16),
            pltpu.VMEM((GROUPS, PAIRS, 128), F32),
            pltpu.VMEM((GROUPS, 2, CHIPS, 64, 128), F32),
            pltpu.VMEM((GROUPS, 2, CHIPS, 64, 128), F32),
            pltpu.VMEM((GROUPS, CHIPS, 2, 64, 128), BF16),
            pltpu.VMEM((GROUPS, CHIPS - 1, 2, 64, 128), BF16),
            pltpu.VMEM((COLS, 32, 128), F32),
            pltpu.VMEM((PAIRS, 128), F32),
            pltpu.VMEM((COLS - 1, 32, 128), BF16),
            pltpu.VMEM((COLS - 1, 32, 128), BF16),
            pltpu.SemaphoreType.DMA((GROUPS, 2)),
            pltpu.SemaphoreType.DMA((GROUPS, 2, PIECES)),
            pltpu.SemaphoreType.DMA,
            pltpu.SemaphoreType.DMA((GROUPS, 2)),
            pltpu.SemaphoreType.DMA((GROUPS, 2)),
            pltpu.SemaphoreType.DMA((GROUPS,)),
            pltpu.SemaphoreType.DMA((GROUPS,)),
            pltpu.SemaphoreType.DMA,
            pltpu.SemaphoreType.DMA,
        ],
        compiler_params=pltpu.CompilerParams(
            collective_id=0, has_side_effects=True, vmem_limit_bytes=56 * 2**20),
        cost_estimate=pl.CostEstimate(flops=13 * 10**9, bytes_accessed=13 * 10**6, transcendentals=0),
    )(integrals, amplitudes)
    return jnp.transpose(out.reshape(VB, 2, 2, OB), (1, 0, 2, 3))


def solution(mesh):
    return jax.shard_map(
        shards,
        mesh=mesh,
        in_specs=(P("row", "col", None), P("row", "col")),
        out_specs=P("col", None, "row", None),
        check_vma=False,
    )
```

```python
import jax
import jax.numpy as jnp
from jax import lax
from jax.experimental import pallas as pl
from jax.experimental.pallas import tpu as pltpu
from jax.sharding import PartitionSpec as P

MESH = pl.DeviceIdType.MESH
F32 = jnp.float32
BF16 = jnp.bfloat16

ROWS = 16
CHIPS = 8
COLS = 16
CW = 56
DW = 56
VB = 32
OB = 32
PAIRS = OB * OB
GROUPS = 8
PIECES = 7
LANES = DW * VB // PIECES
TILES = LANES // 128
KP = TILES * 256


def kernel(w_ref, t_ref, o_ref, wbuf, tbuf, lhs, rhs, acc, core_in, row_out, row_in, own, swap_out, swap_in, turn, crossed, direct, mirror,
           col_out, col_in, w_send, w_recv, t_sem, core_send, core_recv, row_send, row_recv, swap_send, swap_recv, col_send, col_recv):
    r = lax.axis_index("row")
    q = lax.axis_index("col")
    z, y = q // 2, q % 2
    u, c = r // 2, r % 2

    def step(g, h):
        i = g % 4
        far = (i + 3) // 4
        dz = (1 - far) * 4 * (1 - h) + far * (4 - i) * (1 - 2 * h)
        return dz, 1 - g // 4

    def target(g, h):
        dz, dy = step(g, h)
        return lax.rem(z + dz + 8, 8) * 2 + lax.rem(y + dy, 2)

    def origin(g, h):
        dz, dy = step(g, h)
        return lax.rem(z - dz + 8, 8) * 2 + lax.rem(y - dy + 2, 2)

    def piece(g, h, k):
        return wbuf.at[g * 2 + h, :, :, pl.ds(pl.multiple_of(k * LANES, 128), LANES)]

    def send_piece(g, h, k):
        p = target(g, h)
        columns = pl.ds(pl.multiple_of(p * (DW * VB) + k * LANES, 128), LANES)
        return pltpu.make_async_remote_copy(
            src_ref=w_ref.at[:, :, columns], dst_ref=piece(g, h, k),
            send_sem=w_send.at[g, h], recv_sem=w_recv.at[g, h, k],
            device_id=(r, p), device_id_type=MESH)

    def local_copy(k):
        columns = pl.ds(pl.multiple_of(q * (DW * VB) + k * LANES, 128), LANES)
        return pltpu.make_async_copy(w_ref.at[:, :, columns], piece(4, 1, k), w_recv.at[4, 1, k])

    t_copy = pltpu.make_async_copy(t_ref, tbuf, t_sem)
    t_copy.start()

    barrier = pltpu.get_barrier_semaphore()
    for k in range(1, COLS):
        pl.semaphore_signal(barrier, inc=1, device_id=(r, lax.rem(q + k, COLS)), device_id_type=MESH)
    for k in range(1, ROWS):
        pl.semaphore_signal(barrier, inc=1, device_id=(lax.rem(r + k, ROWS), q), device_id_type=MESH)
    pl.semaphore_wait(barrier, COLS + ROWS - 2)

    for slot in range(2 * GROUPS + PIECES - 2):
        @pl.loop(max(0, slot - PIECES + 2) // 2, min(GROUPS - 1, slot // 2) + 1)
        def _(g):
            send_piece(g, 0, slot - 2 * g).start()

            @pl.when(g != 4)
            def _():
                send_piece(g, 1, slot - 2 * g).start()

    @pl.loop(0, PIECES)
    def _(k):
        local_copy(k).start()

    t_copy.wait()
    gap = jnp.zeros((8, PAIRS), F32)

    @pl.loop(0, PIECES)
    def _(k):
        for n in range(KP // 128):
            base = pl.multiple_of((k * (KP // 128) + n) * 2 * PAIRS, 128)
            first = tbuf[:, pl.ds(base, PAIRS)].astype(F32)
            second = tbuf[:, pl.ds(base + PAIRS, PAIRS)].astype(F32)
            both = jnp.concatenate([first, gap, second, gap], axis=0)
            lhs[k, :, n * 128:(n + 1) * 128] = both.T.astype(BF16)

    @pl.loop(0, GROUPS)
    def _(g):
        acc[g] = jnp.zeros((PAIRS, 128), F32)
        swap_out[g] = jnp.zeros((ROWS, 8, 128), F32)

    quarter = lax.broadcasted_iota(jnp.int32, (CW, 128), 1) // 32
    pad = jnp.zeros((8, 128), F32)

    def compute(g, k):
        for h in range(2):
            pltpu.make_async_copy(piece(g, h, k), piece(g, h, k), w_recv.at[g, h, k]).wait()
        for t in range(TILES):
            columns = pl.ds(pl.multiple_of(k * LANES + t * 128, 128), 128)
            x = [wbuf[g * 2 + h, :, :, columns].astype(F32) for h in range(2)]
            x = [x[h][:, a, :] for h in range(2) for a in range(2)]
            for d in range(4):
                out = None
                for n in range(4):
                    moved = pltpu.roll(x[n], (n - d) % 4 * 32, 1) if n != d else x[n]
                    out = jnp.where(quarter == n, moved, out) if n else moved
                rhs[t * 256 + d * 64:t * 256 + (d + 1) * 64] = (
                    jnp.concatenate([out, pad], axis=0).astype(BF16))
        acc[g] += jnp.dot(lhs[k], rhs[...], preferred_element_type=F32)

    def mine(p, core):
        return pl.ds(pl.multiple_of((p * 2 + core) * 64, 64), 64)

    def scatter(g):
        @pl.loop(0, CHIPS, unroll=True)
        def _(p):
            pltpu.make_async_remote_copy(
                src_ref=acc.at[g, mine(p, 1 - c)], dst_ref=core_in.at[g, p],
                send_sem=core_send.at[g], recv_sem=core_recv.at[g],
                device_id=(r + 1 - 2 * c, q), device_id_type=MESH).start()

    def pair(g):
        pltpu.make_async_copy(core_in.at[g], core_in.at[g], core_recv.at[g]).wait()

        @pl.loop(1, CHIPS, unroll=True)
        def _(k):
            p = lax.rem(u + k, CHIPS)
            row_out[g, p] = (acc[g, mine(p, c)] + core_in[g, p]).astype(BF16)
            pltpu.make_async_remote_copy(
                src_ref=row_out.at[g, p], dst_ref=row_in.at[g, k - 1],
                send_sem=row_send.at[g], recv_sem=row_recv.at[g],
                device_id=(p * 2 + c, q), device_id_type=MESH).start()

    def column(g):
        straight = acc[g, mine(u, c)] + core_in[g, u]
        pltpu.make_async_copy(row_in.at[g], row_in.at[g], row_recv.at[g]).wait()
        for k in range(CHIPS - 1):
            straight += row_in[g, k].astype(F32)
        own[g] = straight
        for p in range(ROWS):
            swap_out[g, p, 0:2] = straight[2 * p:2 * p + 2]
            swap_out[g, p, 2:4] = straight[OB + 2 * p:OB + 2 * p + 2]

        @pl.loop(1, ROWS, unroll=5)
        def _(k):
            p = lax.rem(r + k, ROWS)
            pltpu.make_async_remote_copy(
                src_ref=swap_out.at[g, p], dst_ref=swap_in.at[g, r],
                send_sem=swap_send.at[g], recv_sem=swap_recv.at[g],
                device_id=(p, q), device_id_type=MESH).start()

        swap_in[g, r] = swap_out[g, r]

    low = lax.broadcasted_iota(jnp.int32, (32, 128), 1) < 64

    def collect(g):
        pltpu.make_async_copy(swap_in.at[g, 1:ROWS], swap_in.at[g, 1:ROWS], swap_recv.at[g]).wait()
        flat = swap_in[g].reshape(ROWS * 8, 128)
        turn[...] = flat
        for j in range(2):
            for i in range(2):
                crossed[pl.ds(j * OB + i, ROWS, stride=2), :] = turn[pl.ds(2 * i + j, ROWS, stride=8), :]
        turned = jnp.concatenate([own[g], crossed[...]], axis=0).T
        for h in range(2):
            p = origin(g, h)
            x0 = turned[h * 64:h * 64 + 32]
            x1 = turned[h * 64 + 32:h * 64 + 64]
            direct[p] = jnp.where(low, x0, pltpu.roll(x1, 64, 1))
            mirror[pl.ds(pl.multiple_of(p * 64, 64), 64), :] = turned[h * 64:h * 64 + 64]

    @pl.loop(0, GROUPS)
    def _(g):
        @pl.loop(0, PIECES)
        def _(k):
            compute(g, k)

            early = 2 * (g - GROUPS // 2)
            for n in range(2):
                late = (g >= GROUPS // 2) & (early + n < GROUPS - 1)

                @pl.when((k == n) & late)
                def _():
                    pair(early + n)

                @pl.when((k == 2 + n) & late)
                def _():
                    column(early + n)

                @pl.when((k == 4 + n) & late)
                def _():
                    collect(early + n)

        scatter(g)

    pair(GROUPS - 1)
    column(GROUPS - 1)
    collect(GROUPS - 1)

    def finish(p):
        x0 = mirror[pl.ds(2 * p, 32, stride=32), :]
        x1 = mirror[pl.ds(2 * p + 1, 32, stride=32), :]
        return direct[p] + jnp.where(low, pltpu.roll(x0, 64, 1), x1)

    @pl.loop(1, COLS, unroll=5)
    def _(k):
        p = lax.rem(q + k, COLS)
        col_out[k - 1] = finish(p).astype(BF16)
        pltpu.make_async_remote_copy(
            src_ref=col_out.at[k - 1], dst_ref=col_in.at[k - 1],
            send_sem=col_send, recv_sem=col_recv,
            device_id=(r, p), device_id_type=MESH).start()

    total = finish(q)
    pltpu.make_async_copy(col_in, col_in, col_recv).wait()
    for k in range(COLS - 1):
        total += col_in[k].astype(F32)
    o_ref[...] = total.astype(BF16)

    pltpu.make_async_copy(col_out, col_out, col_send).wait()

    @pl.loop(0, GROUPS)
    def _(g):
        pltpu.make_async_copy(core_in.at[g], core_in.at[g], core_send.at[g]).wait()
        pltpu.make_async_copy(swap_in.at[g, 1:ROWS], swap_in.at[g, 1:ROWS], swap_send.at[g]).wait()
        pltpu.make_async_copy(row_in.at[g], row_in.at[g], row_send.at[g]).wait()
        pltpu.make_async_copy(wbuf.at[g * 2], wbuf.at[g * 2], w_send.at[g, 0]).wait()

        @pl.when(g != 4)
        def _():
            pltpu.make_async_copy(wbuf.at[g * 2 + 1], wbuf.at[g * 2 + 1], w_send.at[g, 1]).wait()


def shards(integrals, amplitudes):
    out = pl.pallas_call(
        kernel,
        out_shape=jax.ShapeDtypeStruct((VB, 128), BF16),
        in_specs=[pl.BlockSpec(memory_space=pl.ANY)] * 2,
        out_specs=pl.BlockSpec(memory_space=pltpu.VMEM),
        scratch_shapes=[
            pltpu.VMEM((2 * GROUPS, CW, 2, DW * VB), BF16),
            pltpu.VMEM((CW, DW * PAIRS), BF16),
            pltpu.VMEM((PIECES, PAIRS, KP), BF16),
            pltpu.VMEM((KP, 128), BF16),
            pltpu.VMEM((GROUPS, PAIRS, 128), F32),
            pltpu.VMEM((GROUPS, CHIPS, 64, 128), F32),
            pltpu.VMEM((GROUPS, CHIPS, 64, 128), BF16),
            pltpu.VMEM((GROUPS, CHIPS - 1, 64, 128), BF16),
            pltpu.VMEM((GROUPS, 64, 128), F32),
            pltpu.VMEM((GROUPS, ROWS, 8, 128), F32),
            pltpu.VMEM((GROUPS, ROWS, 8, 128), F32),
            pltpu.VMEM((ROWS * 8, 128), F32),
            pltpu.VMEM((64, 128), F32),
            pltpu.VMEM((COLS, 32, 128), F32),
            pltpu.VMEM((PAIRS, 128), F32),
            pltpu.VMEM((COLS - 1, 32, 128), BF16),
            pltpu.VMEM((COLS - 1, 32, 128), BF16),
            pltpu.SemaphoreType.DMA((GROUPS, 2)),
            pltpu.SemaphoreType.DMA((GROUPS, 2, PIECES)),
            pltpu.SemaphoreType.DMA,
            pltpu.SemaphoreType.DMA((GROUPS,)),
            pltpu.SemaphoreType.DMA((GROUPS,)),
            pltpu.SemaphoreType.DMA((GROUPS,)),
            pltpu.SemaphoreType.DMA((GROUPS,)),
            pltpu.SemaphoreType.DMA((GROUPS,)),
            pltpu.SemaphoreType.DMA((GROUPS,)),
            pltpu.SemaphoreType.DMA,
            pltpu.SemaphoreType.DMA,
        ],
        compiler_params=pltpu.CompilerParams(
            collective_id=0, has_side_effects=True, vmem_limit_bytes=56 * 2**20),
        cost_estimate=pl.CostEstimate(flops=13 * 10**9, bytes_accessed=13 * 10**6, transcendentals=0),
    )(integrals, amplitudes)
    return jnp.transpose(out.reshape(VB, 2, 2, OB), (1, 0, 2, 3))


def solution(mesh):
    return jax.shard_map(
        shards,
        mesh=mesh,
        in_specs=(P("row", "col", None), P("row", "col")),
        out_specs=P("col", None, "row", None),
        check_vma=False,
    )
```

```python
import jax
import jax.numpy as jnp
from jax import lax
from jax.experimental import pallas as pl
from jax.experimental.pallas import tpu as pltpu
from jax.sharding import PartitionSpec as P

MESH = pl.DeviceIdType.MESH
F32 = jnp.float32
BF16 = jnp.bfloat16

ROWS = 16
CHIPS = 8
COLS = 16
CW = 56
DW = 56
VB = 32
FAR = [(dz, dy) for dz in range(8) for dy in range(2)]
OB = 32
PAIRS = OB * OB
GROUPS = 8
PIECES = 7
LANES = DW * VB // PIECES
TILES = LANES // 128
KP = TILES * 256


def kernel(w_ref, t_ref, o_ref, wbuf, tbuf, lhs, rhs, acc, cross, core_in, row_out, row_in, direct, mirror,
           col_out, col_in, w_send, w_recv, t_sem, core_send, core_recv, row_send, row_recv, col_send, col_recv):
    r = lax.axis_index("row")
    q = lax.axis_index("col")
    z, y = q // 2, q % 2
    u, c = r // 2, r % 2

    def step(g, h):
        n = g % 4
        i = n + g // 4 * (3 - 2 * n + n // 2 * (2 * n - 5))
        far = (i + 3) // 4
        dz = (1 - far) * 4 * (1 - h) + far * (4 - i) * (1 - 2 * h)
        return dz, 1 - g // 4

    def target(g, h):
        dz, dy = step(g, h)
        return lax.rem(z + dz + 8, 8) * 2 + lax.rem(y + dy, 2)

    def origin(g, h):
        dz, dy = step(g, h)
        return lax.rem(z - dz + 8, 8) * 2 + lax.rem(y - dy + 2, 2)

    def piece(g, h, k):
        return wbuf.at[g * 2 + h, :, :, pl.ds(pl.multiple_of(k * LANES, 128), LANES)]

    def send_piece(g, h, k):
        p = target(g, h)
        columns = pl.ds(pl.multiple_of(p * (DW * VB) + k * LANES, 128), LANES)
        return pltpu.make_async_remote_copy(
            src_ref=w_ref.at[:, :, columns], dst_ref=piece(g, h, k),
            send_sem=w_send.at[g, h], recv_sem=w_recv.at[g, h, k],
            device_id=(r, p), device_id_type=MESH)

    def local_copy(k):
        columns = pl.ds(pl.multiple_of(q * (DW * VB) + k * LANES, 128), LANES)
        return pltpu.make_async_copy(w_ref.at[:, :, columns], piece(6, 1, k), w_recv.at[6, 1, k])

    t_copy = pltpu.make_async_copy(t_ref, tbuf, t_sem)
    t_copy.start()

    barrier = pltpu.get_barrier_semaphore()
    for k in range(1, COLS):
        pl.semaphore_signal(barrier, inc=1, device_id=(r, lax.rem(q + k, COLS)), device_id_type=MESH)
    for k in range(1, ROWS):
        pl.semaphore_signal(barrier, inc=1, device_id=(lax.rem(r + k, ROWS), q), device_id_type=MESH)
    pl.semaphore_wait(barrier, COLS + ROWS - 2)

    for slot in range(2 * GROUPS + PIECES - 2):
        @pl.loop(max(0, slot - PIECES + 2) // 2, min(GROUPS - 1, slot // 2) + 1)
        def _(g):
            send_piece(g, 0, slot - 2 * g).start()

            @pl.when(g != 6)
            def _():
                send_piece(g, 1, slot - 2 * g).start()

    @pl.loop(0, PIECES)
    def _(k):
        local_copy(k).start()

    t_copy.wait()
    gap = jnp.zeros((8, PAIRS), F32)

    @pl.loop(0, PIECES)
    def _(k):
        for n in range(KP // 128):
            base = pl.multiple_of((k * (KP // 128) + n) * 2 * PAIRS, 128)
            first = tbuf[:, pl.ds(base, PAIRS)].astype(F32)
            second = tbuf[:, pl.ds(base + PAIRS, PAIRS)].astype(F32)
            both = jnp.concatenate([first, gap, second, gap], axis=0)
            lhs[k, :, n * 128:(n + 1) * 128] = both.T.astype(BF16)

    @pl.loop(0, GROUPS)
    def _(g):
        acc[g] = jnp.zeros((PAIRS, 128), F32)

    quarter = lax.broadcasted_iota(jnp.int32, (CW, 128), 1) // 32
    pad = jnp.zeros((8, 128), F32)

    def compute(g, k):
        for h in range(2):
            pltpu.make_async_copy(piece(g, h, k), piece(g, h, k), w_recv.at[g, h, k]).wait()
        for t in range(TILES):
            columns = pl.ds(pl.multiple_of(k * LANES + t * 128, 128), 128)
            x = [wbuf[g * 2 + h, :, :, columns].astype(F32) for h in range(2)]
            x = [x[h][:, a, :] for h in range(2) for a in range(2)]
            for d in range(4):
                out = None
                for n in range(4):
                    moved = pltpu.roll(x[n], (n - d) % 4 * 32, 1) if n != d else x[n]
                    out = jnp.where(quarter == n, moved, out) if n else moved
                rhs[t * 256 + d * 64:t * 256 + (d + 1) * 64] = (
                    jnp.concatenate([out, pad], axis=0).astype(BF16))
        acc[g] += jnp.dot(lhs[k], rhs[...], preferred_element_type=F32)

    def cross_copy(g):
        return pltpu.make_async_remote_copy(
            src_ref=cross.at[g, 1 - c], dst_ref=core_in.at[g, 1],
            send_sem=core_send.at[g, 1], recv_sem=core_recv.at[g, 1],
            device_id=(r + 1 - 2 * c, q), device_id_type=MESH)

    def mine(p, core):
        return pl.ds(pl.multiple_of((p * 2 + core) * 64, 64), 64)

    def scatter(g):
        @pl.loop(0, CHIPS)
        def _(p):
            pltpu.make_async_remote_copy(
                src_ref=acc.at[g, mine(p, 1 - c)], dst_ref=core_in.at[g, 0, p],
                send_sem=core_send.at[g, 0], recv_sem=core_recv.at[g, 0],
                device_id=(r + 1 - 2 * c, q), device_id_type=MESH).start()

        for j in range(OB):
            cross[g, j // 2 % 2, j // 4, j % 2 * 32:(j % 2 + 1) * 32] = acc[g, pl.ds(j, 32, stride=32), :]
        cross_copy(g).start()

    def pair(g):
        pltpu.make_async_copy(core_in.at[g, 0], core_in.at[g, 0], core_recv.at[g, 0]).wait()
        cross_copy(g).wait_recv()

        for k, (dy, dx) in enumerate(((1, 2), (1, 1), (1, 3), (0, 2), (1, 0), (0, 1), (0, 3))):
            p = lax.rem(u // 4 + dy, 2) * 4 + lax.rem(u + dx, 4)
            row_out[g, p, 0] = (acc[g, mine(p, c)] + core_in[g, 0, p]).astype(BF16)
            row_out[g, p, 1] = (cross[g, c, p] + core_in[g, 1, p]).astype(BF16)
            pltpu.make_async_remote_copy(
                src_ref=row_out.at[g, p], dst_ref=row_in.at[g, k],
                send_sem=row_send.at[g], recv_sem=row_recv.at[g],
                device_id=(p * 2 + c, q), device_id_type=MESH).start()

    low = lax.broadcasted_iota(jnp.int32, (32, 128), 1) < 64

    def collect(g):
        straight = acc[g, mine(u, c)] + core_in[g, 0, u]
        crossed = cross[g, c, u] + core_in[g, 1, u]
        pltpu.make_async_copy(row_in.at[g], row_in.at[g], row_recv.at[g]).wait()
        for k in range(CHIPS - 1):
            straight += row_in[g, k, 0].astype(F32)
            crossed += row_in[g, k, 1].astype(F32)
        turned = jnp.concatenate([straight, crossed], axis=0).T
        for h in range(2):
            p = origin(g, h)
            x0 = turned[h * 64:h * 64 + 32]
            x1 = turned[h * 64 + 32:h * 64 + 64]
            direct[p] = jnp.where(low, x0, pltpu.roll(x1, 64, 1))
            mirror[pl.ds(pl.multiple_of(p * 64, 64), 64), :] = turned[h * 64:h * 64 + 64]

    @pl.loop(0, GROUPS)
    def _(g):
        @pl.loop(0, PIECES)
        def _(k):
            compute(g, k)

            early = 2 * (g - GROUPS // 2)
            for n in range(2):
                @pl.when((k == 1 + n) & (g >= GROUPS // 2) & (early + n < GROUPS - 1))
                def _():
                    pair(early + n)

                @pl.when((k == 4 + n) & (g >= GROUPS // 2) & (early + n < GROUPS - 2))
                def _():
                    collect(early + n)

        scatter(g)

    collect(GROUPS - 2)
    pair(GROUPS - 1)
    collect(GROUPS - 1)

    def finish(p):
        x0 = mirror[pl.ds(2 * p, 32, stride=32), :]
        x1 = mirror[pl.ds(2 * p + 1, 32, stride=32), :]
        return direct[p] + jnp.where(low, pltpu.roll(x0, 64, 1), x1)

    far = [(dz, dy) for d in range(5, 0, -1) for dz, dy in FAR if min(dz, 8 - dz) + dy == d]
    for k, (dz, dy) in enumerate(far):
        p = lax.rem(z + dz, 8) * 2 + lax.rem(y + dy, 2)
        col_out[k] = finish(p).astype(BF16)
        pltpu.make_async_remote_copy(
            src_ref=col_out.at[k], dst_ref=col_in.at[k],
            send_sem=col_send, recv_sem=col_recv,
            device_id=(r, p), device_id_type=MESH).start()

    total = finish(q)
    pltpu.make_async_copy(col_in, col_in, col_recv).wait()
    for k in range(COLS - 1):
        total += col_in[k].astype(F32)
    for a in range(2):
        halves = [total[:, a * 64 + i * 32:a * 64 + (i + 1) * 32] for i in range(2)]
        o_ref[a] = jnp.stack(halves, axis=1).astype(BF16)

    pltpu.make_async_copy(col_out, col_out, col_send).wait()

    @pl.loop(0, GROUPS)
    def _(g):
        pltpu.make_async_copy(core_in.at[g, 0], core_in.at[g, 0], core_send.at[g, 0]).wait()
        cross_copy(g).wait_send()
        pltpu.make_async_copy(row_in.at[g], row_in.at[g], row_send.at[g]).wait()
        pltpu.make_async_copy(wbuf.at[g * 2], wbuf.at[g * 2], w_send.at[g, 0]).wait()

        @pl.when(g != 6)
        def _():
            pltpu.make_async_copy(wbuf.at[g * 2 + 1], wbuf.at[g * 2 + 1], w_send.at[g, 1]).wait()


def shards(integrals, amplitudes):
    out = pl.pallas_call(
        kernel,
        out_shape=jax.ShapeDtypeStruct((2, VB, 2, OB), BF16),
        in_specs=[pl.BlockSpec(memory_space=pl.ANY)] * 2,
        out_specs=pl.BlockSpec(memory_space=pltpu.VMEM),
        scratch_shapes=[
            pltpu.VMEM((2 * GROUPS, CW, 2, DW * VB), BF16),
            pltpu.VMEM((CW, DW * PAIRS), BF16),
            pltpu.VMEM((PIECES, PAIRS, KP), BF16),
            pltpu.VMEM((KP, 128), BF16),
            pltpu.VMEM((GROUPS, PAIRS, 128), F32),
            pltpu.VMEM((GROUPS, 2, CHIPS, 64, 128), F32),
            pltpu.VMEM((GROUPS, 2, CHIPS, 64, 128), F32),
            pltpu.VMEM((GROUPS, CHIPS, 2, 64, 128), BF16),
            pltpu.VMEM((GROUPS, CHIPS - 1, 2, 64, 128), BF16),
            pltpu.VMEM((COLS, 32, 128), F32),
            pltpu.VMEM((PAIRS, 128), F32),
            pltpu.VMEM((COLS - 1, 32, 128), BF16),
            pltpu.VMEM((COLS - 1, 32, 128), BF16),
            pltpu.SemaphoreType.DMA((GROUPS, 2)),
            pltpu.SemaphoreType.DMA((GROUPS, 2, PIECES)),
            pltpu.SemaphoreType.DMA,
            pltpu.SemaphoreType.DMA((GROUPS, 2)),
            pltpu.SemaphoreType.DMA((GROUPS, 2)),
            pltpu.SemaphoreType.DMA((GROUPS,)),
            pltpu.SemaphoreType.DMA((GROUPS,)),
            pltpu.SemaphoreType.DMA,
            pltpu.SemaphoreType.DMA,
        ],
        compiler_params=pltpu.CompilerParams(
            collective_id=0, has_side_effects=True, vmem_limit_bytes=56 * 2**20),
        cost_estimate=pl.CostEstimate(flops=13 * 10**9, bytes_accessed=13 * 10**6, transcendentals=0),
    )(integrals, amplitudes)
    return out


def solution(mesh):
    return jax.shard_map(
        shards,
        mesh=mesh,
        in_specs=(P("row", "col", None), P("row", "col")),
        out_specs=P("col", None, "row", None),
        check_vma=False,
    )
```

```python
import jax
import jax.numpy as jnp
from jax import lax
from jax.experimental import pallas as pl
from jax.experimental.pallas import tpu as pltpu
from jax.sharding import PartitionSpec as P

MESH = pl.DeviceIdType.MESH
F32 = jnp.float32
BF16 = jnp.bfloat16

ROWS = 16
CHIPS = 8
COLS = 16
CW = 56
DW = 56
VB = 32
FAR = [(dz, dy) for dz in range(8) for dy in range(2)]
OB = 32
PAIRS = OB * OB
GROUPS = 8
PIECES = 7
LANES = DW * VB // PIECES
TILES = LANES // 128
KP = TILES * 256


def kernel(w_ref, t_ref, o_ref, wbuf, tbuf, lhs, rhs, acc, core_in, row_out, row_in, direct, mirror,
           col_out, col_in, w_send, w_recv, t_sem, core_send, core_recv, row_send, row_recv, col_send, col_recv):
    r = lax.axis_index("row")
    q = lax.axis_index("col")
    z, y = q // 2, q % 2
    u, c = r // 2, r % 2

    def step(g, h):
        n = g % 4
        i = n + g // 4 * (3 - 2 * n + n // 2 * (2 * n - 5))
        far = (i + 3) // 4
        dz = (1 - far) * 4 * (1 - h) + far * (4 - i) * (1 - 2 * h)
        return dz, 1 - g // 4

    def target(g, h):
        dz, dy = step(g, h)
        return lax.rem(z + dz + 8, 8) * 2 + lax.rem(y + dy, 2)

    def origin(g, h):
        dz, dy = step(g, h)
        return lax.rem(z - dz + 8, 8) * 2 + lax.rem(y - dy + 2, 2)

    def piece(g, h, k):
        return wbuf.at[g * 2 + h, :, :, pl.ds(pl.multiple_of(k * LANES, 128), LANES)]

    def send_piece(g, h, k):
        p = target(g, h)
        columns = pl.ds(pl.multiple_of(p * (DW * VB) + k * LANES, 128), LANES)
        return pltpu.make_async_remote_copy(
            src_ref=w_ref.at[:, :, columns], dst_ref=piece(g, h, k),
            send_sem=w_send.at[g, h], recv_sem=w_recv.at[g, h, k],
            device_id=(r, p), device_id_type=MESH)

    def local_copy(k):
        columns = pl.ds(pl.multiple_of(q * (DW * VB) + k * LANES, 128), LANES)
        return pltpu.make_async_copy(w_ref.at[:, :, columns], piece(6, 1, k), w_recv.at[6, 1, k])

    t_copy = pltpu.make_async_copy(t_ref, tbuf, t_sem)
    t_copy.start()

    barrier = pltpu.get_barrier_semaphore()
    for k in range(1, COLS):
        pl.semaphore_signal(barrier, inc=1, device_id=(r, lax.rem(q + k, COLS)), device_id_type=MESH)
    for k in range(1, CHIPS):
        pl.semaphore_signal(barrier, inc=1, device_id=(lax.rem(r + 2 * k, ROWS), q), device_id_type=MESH)
    pl.semaphore_signal(barrier, inc=1, device_id=(r + 1 - 2 * c, q), device_id_type=MESH)
    pl.semaphore_wait(barrier, COLS - 1 + CHIPS)

    for slot in range(2 * GROUPS + PIECES - 2):
        @pl.loop(max(0, slot - PIECES + 2) // 2, min(GROUPS - 1, slot // 2) + 1)
        def _(g):
            send_piece(g, 0, slot - 2 * g).start()

            @pl.when(g != 6)
            def _():
                send_piece(g, 1, slot - 2 * g).start()

    @pl.loop(0, PIECES)
    def _(k):
        local_copy(k).start()

    t_copy.wait()
    gap = jnp.zeros((8, PAIRS), F32)

    @pl.loop(0, PIECES)
    def _(k):
        for n in range(KP // 128):
            base = pl.multiple_of((k * (KP // 128) + n) * 2 * PAIRS, 128)
            first = tbuf[:, pl.ds(base, PAIRS)].astype(F32)
            second = tbuf[:, pl.ds(base + PAIRS, PAIRS)].astype(F32)
            both = jnp.concatenate([first, gap, second, gap], axis=0)
            lhs[k, :, n * 128:(n + 1) * 128] = both.T.astype(BF16)

    @pl.loop(0, GROUPS)
    def _(g):
        acc[g] = jnp.zeros((PAIRS, 128), F32)

    quarter = lax.broadcasted_iota(jnp.int32, (CW, 128), 1) // 32
    pad = jnp.zeros((8, 128), F32)

    def compute(g, k):
        for h in range(2):
            pltpu.make_async_copy(piece(g, h, k), piece(g, h, k), w_recv.at[g, h, k]).wait()
        for t in range(TILES):
            columns = pl.ds(pl.multiple_of(k * LANES + t * 128, 128), 128)
            x = [wbuf[g * 2 + h, :, :, columns].astype(F32) for h in range(2)]
            x = [x[h][:, a, :] for h in range(2) for a in range(2)]
            for d in range(4):
                out = None
                for n in range(4):
                    moved = pltpu.roll(x[n], (n - d) % 4 * 32, 1) if n != d else x[n]
                    out = jnp.where(quarter == n, moved, out) if n else moved
                rhs[t * 256 + d * 64:t * 256 + (d + 1) * 64] = (
                    jnp.concatenate([out, pad], axis=0).astype(BF16))
        acc[g] += jnp.dot(lhs[k], rhs[...], preferred_element_type=F32)

    def core_copy(g):
        return pltpu.make_async_remote_copy(
            src_ref=acc.at[g], dst_ref=core_in.at[g], send_sem=core_send.at[g], recv_sem=core_recv.at[g],
            device_id=(r + 1 - 2 * c, q), device_id_type=MESH)

    def straight_cut(g, p):
        rows = pl.ds(pl.multiple_of((p * 2 + c) * 64, 64), 64)
        return acc[g, rows] + core_in[g, rows]

    def crossed_cut(g, p, n):
        rows = pl.ds((p * 2 + c) * 2 + n, OB, stride=OB)
        return acc[g, rows] + core_in[g, rows]

    def pair(g):
        core_copy(g).wait_recv()
        for k, (dy, dx) in enumerate(((1, 2), (1, 1), (1, 3), (0, 2), (1, 0), (0, 1), (0, 3))):
            p = lax.rem(u // 4 + dy, 2) * 4 + lax.rem(u + dx, 4)
            row_out[g, p, 0] = straight_cut(g, p).astype(BF16)
            for n in range(2):
                row_out[g, p, 1, n * OB:(n + 1) * OB] = crossed_cut(g, p, n).astype(BF16)
            pltpu.make_async_remote_copy(
                src_ref=row_out.at[g, p], dst_ref=row_in.at[g, k],
                send_sem=row_send.at[g], recv_sem=row_recv.at[g],
                device_id=(p * 2 + c, q), device_id_type=MESH).start()

    low = lax.broadcasted_iota(jnp.int32, (32, 128), 1) < 64

    def collect(g):
        straight = straight_cut(g, u)
        crossed = jnp.concatenate([crossed_cut(g, u, n) for n in range(2)], axis=0)
        pltpu.make_async_copy(row_in.at[g], row_in.at[g], row_recv.at[g]).wait()
        for k in range(CHIPS - 1):
            straight += row_in[g, k, 0].astype(F32)
            crossed += row_in[g, k, 1].astype(F32)
        turned = jnp.concatenate([straight, crossed], axis=0).T
        for h in range(2):
            p = origin(g, h)
            x0 = turned[h * 64:h * 64 + 32]
            x1 = turned[h * 64 + 32:h * 64 + 64]
            direct[p] = jnp.where(low, x0, pltpu.roll(x1, 64, 1))
            mirror[pl.ds(pl.multiple_of(p * 64, 64), 64), :] = turned[h * 64:h * 64 + 64]

    @pl.loop(0, GROUPS)
    def _(g):
        @pl.loop(0, PIECES)
        def _(k):
            compute(g, k)

            early = 2 * (g - GROUPS // 2)
            for n in range(2):
                @pl.when((k == 1 + n) & (g >= GROUPS // 2) & (early + n < GROUPS - 1))
                def _():
                    pair(early + n)

                @pl.when((k == 4 + n) & (g >= GROUPS // 2) & (early + n < GROUPS - 2))
                def _():
                    collect(early + n)

        core_copy(g).start()

    collect(GROUPS - 2)
    pair(GROUPS - 1)
    collect(GROUPS - 1)

    def finish(p):
        x0 = mirror[pl.ds(2 * p, 32, stride=32), :]
        x1 = mirror[pl.ds(2 * p + 1, 32, stride=32), :]
        return direct[p] + jnp.where(low, pltpu.roll(x0, 64, 1), x1)

    far = [(dz, dy) for d in range(5, 0, -1) for dz, dy in FAR if min(dz, 8 - dz) + dy == d]
    for k, (dz, dy) in enumerate(far):
        p = lax.rem(z + dz, 8) * 2 + lax.rem(y + dy, 2)
        col_out[k] = finish(p).astype(BF16)
        pltpu.make_async_remote_copy(
            src_ref=col_out.at[k], dst_ref=col_in.at[k],
            send_sem=col_send, recv_sem=col_recv,
            device_id=(r, p), device_id_type=MESH).start()

    total = finish(q)
    pltpu.make_async_copy(col_in, col_in, col_recv).wait()
    for k in range(COLS - 1):
        total += col_in[k].astype(F32)
    for a in range(2):
        halves = [total[:, a * 64 + i * 32:a * 64 + (i + 1) * 32] for i in range(2)]
        o_ref[a] = jnp.stack(halves, axis=1).astype(BF16)

    pltpu.make_async_copy(col_out, col_out, col_send).wait()

    @pl.loop(0, GROUPS)
    def _(g):
        core_copy(g).wait_send()
        pltpu.make_async_copy(row_in.at[g], row_in.at[g], row_send.at[g]).wait()
        pltpu.make_async_copy(wbuf.at[g * 2], wbuf.at[g * 2], w_send.at[g, 0]).wait()

        @pl.when(g != 6)
        def _():
            pltpu.make_async_copy(wbuf.at[g * 2 + 1], wbuf.at[g * 2 + 1], w_send.at[g, 1]).wait()


def shards(integrals, amplitudes):
    out = pl.pallas_call(
        kernel,
        out_shape=jax.ShapeDtypeStruct((2, VB, 2, OB), BF16),
        in_specs=[pl.BlockSpec(memory_space=pl.ANY)] * 2,
        out_specs=pl.BlockSpec(memory_space=pltpu.VMEM),
        scratch_shapes=[
            pltpu.VMEM((2 * GROUPS, CW, 2, DW * VB), BF16),
            pltpu.VMEM((CW, DW * PAIRS), BF16),
            pltpu.VMEM((PIECES, PAIRS, KP), BF16),
            pltpu.VMEM((KP, 128), BF16),
            pltpu.VMEM((GROUPS, PAIRS, 128), F32),
            pltpu.VMEM((GROUPS, PAIRS, 128), F32),
            pltpu.VMEM((GROUPS, CHIPS, 2, 64, 128), BF16),
            pltpu.VMEM((GROUPS, CHIPS - 1, 2, 64, 128), BF16),
            pltpu.VMEM((COLS, 32, 128), F32),
            pltpu.VMEM((PAIRS, 128), F32),
            pltpu.VMEM((COLS - 1, 32, 128), BF16),
            pltpu.VMEM((COLS - 1, 32, 128), BF16),
            pltpu.SemaphoreType.DMA((GROUPS, 2)),
            pltpu.SemaphoreType.DMA((GROUPS, 2, PIECES)),
            pltpu.SemaphoreType.DMA,
            pltpu.SemaphoreType.DMA((GROUPS,)),
            pltpu.SemaphoreType.DMA((GROUPS,)),
            pltpu.SemaphoreType.DMA((GROUPS,)),
            pltpu.SemaphoreType.DMA((GROUPS,)),
            pltpu.SemaphoreType.DMA,
            pltpu.SemaphoreType.DMA,
        ],
        compiler_params=pltpu.CompilerParams(
            collective_id=0, has_side_effects=True, vmem_limit_bytes=56 * 2**20),
        cost_estimate=pl.CostEstimate(flops=13 * 10**9, bytes_accessed=13 * 10**6, transcendentals=0),
    )(integrals, amplitudes)
    return out


def solution(mesh):
    return jax.shard_map(
        shards,
        mesh=mesh,
        in_specs=(P("row", "col", None), P("row", "col")),
        out_specs=P("col", None, "row", None),
        check_vma=False,
    )
```

```python
import jax
import jax.numpy as jnp
from jax import lax
from jax.experimental import pallas as pl
from jax.experimental.pallas import tpu as pltpu
from jax.sharding import PartitionSpec as P

MESH = pl.DeviceIdType.MESH
F32 = jnp.float32
BF16 = jnp.bfloat16

ROWS = 16
CHIPS = 8
COLS = 16
CW = 56
DW = 56
VB = 32
FAR = [(dz, dy) for dz in range(8) for dy in range(2)]
OB = 32
PAIRS = OB * OB
SPAN = PAIRS + OB
GROUPS = 8
PIECES = 7
LANES = DW * VB // PIECES
TILES = LANES // 128
KP = TILES * 256


def kernel(w_ref, t_ref, o_ref, wbuf, tbuf, lhs, rhs, acc, core_in, row_out, row_in, direct, mirror,
           col_out, col_in, w_send, w_recv, t_sem, core_send, core_recv, row_send, row_recv, col_send, col_recv):
    r = lax.axis_index("row")
    q = lax.axis_index("col")
    z, y = q // 2, q % 2
    u, c = r // 2, r % 2

    def step(g, h):
        n = g % 4
        i = n + g // 4 * (3 - 2 * n + n // 2 * (2 * n - 5))
        far = (i + 3) // 4
        dz = (1 - far) * 4 * (1 - h) + far * (4 - i) * (1 - 2 * h)
        return dz, 1 - g // 4

    def target(g, h):
        dz, dy = step(g, h)
        return lax.rem(z + dz + 8, 8) * 2 + lax.rem(y + dy, 2)

    def origin(g, h):
        dz, dy = step(g, h)
        return lax.rem(z - dz + 8, 8) * 2 + lax.rem(y - dy + 2, 2)

    def piece(g, h, k):
        return wbuf.at[g * 2 + h, :, :, pl.ds(pl.multiple_of(k * LANES, 128), LANES)]

    def send_piece(g, h, k):
        p = target(g, h)
        columns = pl.ds(pl.multiple_of(p * (DW * VB) + k * LANES, 128), LANES)
        return pltpu.make_async_remote_copy(
            src_ref=w_ref.at[:, :, columns], dst_ref=piece(g, h, k),
            send_sem=w_send.at[g, h], recv_sem=w_recv.at[g, h, k],
            device_id=(r, p), device_id_type=MESH)

    def local_copy(k):
        columns = pl.ds(pl.multiple_of(q * (DW * VB) + k * LANES, 128), LANES)
        return pltpu.make_async_copy(w_ref.at[:, :, columns], piece(6, 1, k), w_recv.at[6, 1, k])

    t_copy = pltpu.make_async_copy(t_ref, tbuf, t_sem)
    t_copy.start()

    barrier = pltpu.get_barrier_semaphore()
    for k in (9, 7, 8, 10, 6, 11, 5, 12, 4, 13, 3, 14, 2, 15, 1):
        pl.semaphore_signal(barrier, inc=1, device_id=(r, lax.rem(q + k, COLS)), device_id_type=MESH)
    for k in range(1, CHIPS):
        pl.semaphore_signal(barrier, inc=1, device_id=(lax.rem(r + 2 * k, ROWS), q), device_id_type=MESH)
    pl.semaphore_signal(barrier, inc=1, device_id=(r + 1 - 2 * c, q), device_id_type=MESH)
    pl.semaphore_wait(barrier, COLS - 1 + CHIPS)

    for slot in range(2 * GROUPS + PIECES - 2):
        @pl.loop(max(0, slot - PIECES + 2) // 2, min(GROUPS - 1, slot // 2) + 1)
        def _(g):
            send_piece(g, 0, slot - 2 * g).start()

            @pl.when(g != 6)
            def _():
                send_piece(g, 1, slot - 2 * g).start()

    @pl.loop(0, PIECES)
    def _(k):
        local_copy(k).start()

    t_copy.wait()
    gap = jnp.zeros((8, PAIRS), F32)

    @pl.loop(0, PIECES)
    def _(k):
        for n in range(KP // 128):
            base = pl.multiple_of((k * (KP // 128) + n) * 2 * PAIRS, 128)
            first = tbuf[:, pl.ds(base, PAIRS)].astype(F32)
            second = tbuf[:, pl.ds(base + PAIRS, PAIRS)].astype(F32)
            both = jnp.concatenate([first, gap, second, gap], axis=0)
            lhs[k, :, n * 128:(n + 1) * 128] = both.T.astype(BF16)

    @pl.loop(0, GROUPS)
    def _(g):
        acc[g] = jnp.zeros((SPAN, 128), F32)

    quarter = lax.broadcasted_iota(jnp.int32, (CW, 128), 1) // 32
    pad = jnp.zeros((8, 128), F32)

    def compute(g, k):
        for h in range(2):
            pltpu.make_async_copy(piece(g, h, k), piece(g, h, k), w_recv.at[g, h, k]).wait()
        for t in range(TILES):
            columns = pl.ds(pl.multiple_of(k * LANES + t * 128, 128), 128)
            x = [wbuf[g * 2 + h, :, :, columns].astype(F32) for h in range(2)]
            x = [x[h][:, a, :] for h in range(2) for a in range(2)]
            for d in range(4):
                out = None
                for n in range(4):
                    moved = pltpu.roll(x[n], (n - d) % 4 * 32, 1) if n != d else x[n]
                    out = jnp.where(quarter == n, moved, out) if n else moved
                rhs[t * 256 + d * 64:t * 256 + (d + 1) * 64] = (
                    jnp.concatenate([out, pad], axis=0).astype(BF16))
        acc[g, :PAIRS] += jnp.dot(lhs[k], rhs[...], preferred_element_type=F32)

    def core_copy(g):
        return pltpu.make_async_remote_copy(
            src_ref=acc.at[g, pl.ds(0, PAIRS)], dst_ref=core_in.at[g, pl.ds(0, PAIRS)], send_sem=core_send.at[g], recv_sem=core_recv.at[g],
            device_id=(r + 1 - 2 * c, q), device_id_type=MESH)

    def straight_cut(g, p):
        rows = pl.ds(pl.multiple_of((p * 2 + c) * 64, 64), 64)
        return acc[g, rows] + core_in[g, rows]

    def crossed_cut(g, p, n):
        rows = pl.ds((p * 2 + c) * 2 + n, OB, stride=OB)
        return acc[g, rows] + core_in[g, rows]

    def pair(g):
        core_copy(g).wait_recv()
        for k, (dy, dx) in enumerate(((1, 2), (1, 1), (1, 3), (0, 2), (1, 0), (0, 1), (0, 3))):
            p = lax.rem(u // 4 + dy, 2) * 4 + lax.rem(u + dx, 4)
            row_out[g, p, 0] = straight_cut(g, p).astype(BF16)
            for n in range(2):
                row_out[g, p, 1, n * OB:(n + 1) * OB] = crossed_cut(g, p, n).astype(BF16)
            pltpu.make_async_remote_copy(
                src_ref=row_out.at[g, p], dst_ref=row_in.at[g, k],
                send_sem=row_send.at[g], recv_sem=row_recv.at[g],
                device_id=(p * 2 + c, q), device_id_type=MESH).start()

    low = lax.broadcasted_iota(jnp.int32, (32, 128), 1) < 64

    def collect(g):
        straight = straight_cut(g, u)
        crossed = jnp.concatenate([crossed_cut(g, u, n) for n in range(2)], axis=0)
        pltpu.make_async_copy(row_in.at[g], row_in.at[g], row_recv.at[g]).wait()
        for k in range(CHIPS - 1):
            straight += row_in[g, k, 0].astype(F32)
            crossed += row_in[g, k, 1].astype(F32)
        turned = jnp.concatenate([straight, crossed], axis=0).T
        for h in range(2):
            p = origin(g, h)
            x0 = turned[h * 64:h * 64 + 32]
            x1 = turned[h * 64 + 32:h * 64 + 64]
            direct[p] = jnp.where(low, x0, pltpu.roll(x1, 64, 1))
            mirror[pl.ds(pl.multiple_of(p * 64, 64), 64), :] = turned[h * 64:h * 64 + 64]

    @pl.loop(0, GROUPS)
    def _(g):
        @pl.loop(0, PIECES)
        def _(k):
            compute(g, k)

            early = 2 * (g - GROUPS // 2)
            for n in range(2):
                @pl.when((k == 1 + n) & (g >= GROUPS // 2) & (early + n < GROUPS - 1))
                def _():
                    pair(early + n)

                @pl.when((k == 4 + n) & (g >= GROUPS // 2) & (early + n < GROUPS - 2))
                def _():
                    collect(early + n)

        core_copy(g).start()

    collect(GROUPS - 2)
    pair(GROUPS - 1)
    collect(GROUPS - 1)

    def finish(p):
        x0 = mirror[pl.ds(2 * p, 32, stride=32), :]
        x1 = mirror[pl.ds(2 * p + 1, 32, stride=32), :]
        return direct[p] + jnp.where(low, pltpu.roll(x0, 64, 1), x1)

    far = [(dz, dy) for d in range(5, 0, -1) for dz, dy in FAR if min(dz, 8 - dz) + dy == d]
    for k, (dz, dy) in enumerate(far):
        p = lax.rem(z + dz, 8) * 2 + lax.rem(y + dy, 2)
        col_out[k] = finish(p).astype(BF16)
        pltpu.make_async_remote_copy(
            src_ref=col_out.at[k], dst_ref=col_in.at[k],
            send_sem=col_send, recv_sem=col_recv,
            device_id=(r, p), device_id_type=MESH).start()

    total = finish(q)
    pltpu.make_async_copy(col_in, col_in, col_recv).wait()
    for k in range(COLS - 1):
        total += col_in[k].astype(F32)
    for a in range(2):
        halves = [total[:, a * 64 + i * 32:a * 64 + (i + 1) * 32] for i in range(2)]
        o_ref[a] = jnp.stack(halves, axis=1).astype(BF16)

    pltpu.make_async_copy(col_out, col_out, col_send).wait()

    @pl.loop(0, GROUPS)
    def _(g):
        core_copy(g).wait_send()
        pltpu.make_async_copy(row_in.at[g], row_in.at[g], row_send.at[g]).wait()
        pltpu.make_async_copy(wbuf.at[g * 2], wbuf.at[g * 2], w_send.at[g, 0]).wait()

        @pl.when(g != 6)
        def _():
            pltpu.make_async_copy(wbuf.at[g * 2 + 1], wbuf.at[g * 2 + 1], w_send.at[g, 1]).wait()


def shards(integrals, amplitudes):
    out = pl.pallas_call(
        kernel,
        out_shape=jax.ShapeDtypeStruct((2, VB, 2, OB), BF16),
        in_specs=[pl.BlockSpec(memory_space=pl.ANY)] * 2,
        out_specs=pl.BlockSpec(memory_space=pltpu.VMEM),
        scratch_shapes=[
            pltpu.VMEM((2 * GROUPS, CW, 2, DW * VB), BF16),
            pltpu.VMEM((CW, DW * PAIRS), BF16),
            pltpu.VMEM((PIECES, PAIRS, KP), BF16),
            pltpu.VMEM((KP, 128), BF16),
            pltpu.VMEM((GROUPS, SPAN, 128), F32),
            pltpu.VMEM((GROUPS, SPAN, 128), F32),
            pltpu.VMEM((GROUPS, CHIPS, 2, 64, 128), BF16),
            pltpu.VMEM((GROUPS, CHIPS - 1, 2, 64, 128), BF16),
            pltpu.VMEM((COLS, 32, 128), F32),
            pltpu.VMEM((SPAN, 128), F32),
            pltpu.VMEM((COLS - 1, 32, 128), BF16),
            pltpu.VMEM((COLS - 1, 32, 128), BF16),
            pltpu.SemaphoreType.DMA((GROUPS, 2)),
            pltpu.SemaphoreType.DMA((GROUPS, 2, PIECES)),
            pltpu.SemaphoreType.DMA,
            pltpu.SemaphoreType.DMA((GROUPS,)),
            pltpu.SemaphoreType.DMA((GROUPS,)),
            pltpu.SemaphoreType.DMA((GROUPS,)),
            pltpu.SemaphoreType.DMA((GROUPS,)),
            pltpu.SemaphoreType.DMA,
            pltpu.SemaphoreType.DMA,
        ],
        compiler_params=pltpu.CompilerParams(
            collective_id=0, has_side_effects=True, vmem_limit_bytes=56 * 2**20),
        cost_estimate=pl.CostEstimate(flops=13 * 10**9, bytes_accessed=13 * 10**6, transcendentals=0),
    )(integrals, amplitudes)
    return out


def solution(mesh):
    return jax.shard_map(
        shards,
        mesh=mesh,
        in_specs=(P("row", "col", None), P("row", "col")),
        out_specs=P("col", None, "row", None),
        check_vma=False,
    )
```

```python
import jax
import jax.numpy as jnp
from jax import lax
from jax.experimental import pallas as pl
from jax.experimental.pallas import tpu as pltpu
from jax.sharding import PartitionSpec as P

MESH = pl.DeviceIdType.MESH
F32 = jnp.float32
BF16 = jnp.bfloat16

ROWS = 16
CHIPS = 8
COLS = 16
CW = 56
DW = 56
VB = 32
LAST = 15
FAR = [(dz, dy) for dz in range(8) for dy in range(2)]
OB = 32
PAIRS = OB * OB
SPAN = PAIRS + OB
GROUPS = 8
PIECES = 7
LANES = DW * VB // PIECES
TILES = LANES // 128
KP = TILES * 256


def kernel(w_ref, t_ref, o_ref, wbuf, tbuf, lhs, rhs, acc, core_in, row_out, row_in, direct, mirror, ready, turn,
           col_out, col_in, w_send, w_recv, t_sem, core_send, core_recv, row_send, row_recv, col_send, col_recv):
    r = lax.axis_index("row")
    q = lax.axis_index("col")
    z, y = q // 2, q % 2
    u, c = r // 2, r % 2

    def step(g, h):
        n = g % 4
        i = n + g // 4 * (3 - 2 * n + n // 2 * (2 * n - 5))
        far = (i + 3) // 4
        dz = (1 - far) * 4 * (1 - h) + far * (4 - i) * (1 - 2 * h)
        return dz, 1 - g // 4

    def target(g, h):
        dz, dy = step(g, h)
        return lax.rem(z + dz + 8, 8) * 2 + lax.rem(y + dy, 2)

    def origin(g, h):
        dz, dy = step(g, h)
        return lax.rem(z - dz + 8, 8) * 2 + lax.rem(y - dy + 2, 2)

    def piece(g, h, k):
        return wbuf.at[g * 2 + h, :, :, pl.ds(pl.multiple_of(k * LANES, 128), LANES)]

    def send_piece(g, h, k):
        p = target(g, h)
        columns = pl.ds(pl.multiple_of(p * (DW * VB) + k * LANES, 128), LANES)
        return pltpu.make_async_remote_copy(
            src_ref=w_ref.at[:, :, columns], dst_ref=piece(g, h, k),
            send_sem=w_send.at[g, h], recv_sem=w_recv.at[g, h, k],
            device_id=(r, p), device_id_type=MESH)

    def local_copy(k):
        columns = pl.ds(pl.multiple_of(q * (DW * VB) + k * LANES, 128), LANES)
        return pltpu.make_async_copy(w_ref.at[:, :, columns], piece(6, 1, k), w_recv.at[6, 1, k])

    t_copy = pltpu.make_async_copy(t_ref, tbuf, t_sem)
    t_copy.start()

    barrier = pltpu.get_barrier_semaphore()
    for k in (9, 7, 8, 10, 6, 11, 5, 12, 4, 13, 3, 14, 2, 15, 1):
        pl.semaphore_signal(barrier, inc=1, device_id=(r, lax.rem(q + k, COLS)), device_id_type=MESH)
    for k in range(1, CHIPS):
        pl.semaphore_signal(barrier, inc=1, device_id=(lax.rem(r + 2 * k, ROWS), q), device_id_type=MESH)
    pl.semaphore_signal(barrier, inc=1, device_id=(r + 1 - 2 * c, q), device_id_type=MESH)
    pl.semaphore_wait(barrier, COLS - 1 + CHIPS)

    def send_both(g, k):
        send_piece(g, 0, k).start()

        @pl.when(g != 6)
        def _():
            send_piece(g, 1, k).start()

    for slot in range(LAST + PIECES):
        first, end = max(0, slot - PIECES + 2) // 2, min(GROUPS - 2, slot // 2) + 1
        if first < end:
            @pl.loop(first, end)
            def _(g):
                send_both(g, slot - 2 * g)
        if slot >= LAST:
            send_both(GROUPS - 1, slot - LAST)

    @pl.loop(0, PIECES)
    def _(k):
        local_copy(k).start()

    t_copy.wait()
    gap = jnp.zeros((8, PAIRS), F32)

    @pl.loop(0, PIECES)
    def _(k):
        for n in range(KP // 128):
            base = pl.multiple_of((k * (KP // 128) + n) * 2 * PAIRS, 128)
            first = tbuf[:, pl.ds(base, PAIRS)].astype(F32)
            second = tbuf[:, pl.ds(base + PAIRS, PAIRS)].astype(F32)
            both = jnp.concatenate([first, gap, second, gap], axis=0)
            lhs[k, :, n * 128:(n + 1) * 128] = both.T.astype(BF16)

    @pl.loop(0, GROUPS)
    def _(g):
        acc[g] = jnp.zeros((SPAN, 128), F32)

    direct[...] = jnp.zeros_like(direct)
    mirror[...] = jnp.zeros_like(mirror)

    quarter = lax.broadcasted_iota(jnp.int32, (CW, 128), 1) // 32
    pad = jnp.zeros((8, 128), F32)

    def compute(g, k):
        for h in range(2):
            pltpu.make_async_copy(piece(g, h, k), piece(g, h, k), w_recv.at[g, h, k]).wait()
        for t in range(TILES):
            columns = pl.ds(pl.multiple_of(k * LANES + t * 128, 128), 128)
            x = [wbuf[g * 2 + h, :, :, columns].astype(F32) for h in range(2)]
            x = [x[h][:, a, :] for h in range(2) for a in range(2)]
            for d in range(4):
                out = None
                for n in range(4):
                    moved = pltpu.roll(x[n], (n - d) % 4 * 32, 1) if n != d else x[n]
                    out = jnp.where(quarter == n, moved, out) if n else moved
                rhs[t * 256 + d * 64:t * 256 + (d + 1) * 64] = (
                    jnp.concatenate([out, pad], axis=0).astype(BF16))
        acc[g, :PAIRS] += jnp.dot(lhs[k], rhs[...], preferred_element_type=F32)

    def core_copy(g):
        return pltpu.make_async_remote_copy(
            src_ref=acc.at[g, pl.ds(0, PAIRS)], dst_ref=core_in.at[g, pl.ds(0, PAIRS)], send_sem=core_send.at[g], recv_sem=core_recv.at[g],
            device_id=(r + 1 - 2 * c, q), device_id_type=MESH)

    def straight_cut(g, p):
        rows = pl.ds(pl.multiple_of((p * 2 + c) * 64, 64), 64)
        return acc[g, rows] + core_in[g, rows]

    def crossed_cut(g, p, n):
        rows = pl.ds((p * 2 + c) * 2 + n, OB, stride=OB)
        return acc[g, rows] + core_in[g, rows]

    def pair(g):
        core_copy(g).wait_recv()
        for k, (dy, dx) in enumerate(((1, 2), (1, 1), (1, 3), (0, 2), (1, 0), (0, 1), (0, 3))):
            p = lax.rem(u // 4 + dy, 2) * 4 + lax.rem(u + dx, 4)
            row_out[g, p, 0] = straight_cut(g, p).astype(BF16)
            for n in range(2):
                row_out[g, p, 1, n * OB:(n + 1) * OB] = crossed_cut(g, p, n).astype(BF16)
            pltpu.make_async_remote_copy(
                src_ref=row_out.at[g, p], dst_ref=row_in.at[g, k],
                send_sem=row_send.at[g], recv_sem=row_recv.at[g],
                device_id=(p * 2 + c, q), device_id_type=MESH).start()

    low = lax.broadcasted_iota(jnp.int32, (32, 128), 1) < 64

    def turned(g):
        straight = straight_cut(g, u)
        crossed = jnp.concatenate([crossed_cut(g, u, n) for n in range(2)], axis=0)
        pltpu.make_async_copy(row_in.at[g], row_in.at[g], row_recv.at[g]).wait()
        for k in range(CHIPS - 1):
            straight += row_in[g, k, 0].astype(F32)
            crossed += row_in[g, k, 1].astype(F32)
        return jnp.concatenate([straight, crossed], axis=0).T

    def collect(g):
        x = turned(g)
        for h in range(2):
            p = origin(g, h)
            direct[p] = jnp.where(low, x[h * 64:h * 64 + 32], pltpu.roll(x[h * 64 + 32:h * 64 + 64], 64, 1))
            mirror[pl.ds(pl.multiple_of(p * 64, 64), 64), :] = x[h * 64:h * 64 + 64]

    def tile(p):
        return pl.ds(pl.multiple_of(p * VB, VB), VB)

    def merge():
        @pl.loop(0, COLS, unroll=4)
        def _(p):
            x0 = mirror[pl.ds(2 * p, 32, stride=32), :]
            x1 = mirror[pl.ds(2 * p + 1, 32, stride=32), :]
            ready[tile(p), :] = direct[p] + jnp.where(low, pltpu.roll(x0, 64, 1), x1)

    def collect_last(g):
        x = turned(g)
        turn[:128] = x
        for h in range(2):
            p = origin(g, h)
            ready[tile(p), :] += jnp.where(low, x[h * 64:h * 64 + 32], pltpu.roll(x[h * 64 + 32:h * 64 + 64], 64, 1))
            for a in range(2):
                x0 = turn[pl.ds(h * 64 + a * 32, COLS, stride=2), :]
                x1 = turn[pl.ds(h * 64 + a * 32 + 1, COLS, stride=2), :]
                ready[pl.ds(2 * p + a, COLS, stride=VB), :] += jnp.where(low[:COLS], pltpu.roll(x0, 64, 1), x1)

    @pl.loop(0, GROUPS)
    def _(g):
        @pl.loop(0, PIECES)
        def _(k):
            compute(g, k)

            early = 2 * (g - GROUPS // 2)
            for n in range(2):
                @pl.when((k == 1 + n) & (g >= GROUPS // 2) & (early + n < GROUPS - 1))
                def _():
                    pair(early + n)

                @pl.when((k == 4 + n) & (g >= GROUPS // 2) & (early + n < GROUPS - 2))
                def _():
                    collect(early + n)

        core_copy(g).start()

    collect(GROUPS - 2)
    pair(GROUPS - 1)
    merge()
    collect_last(GROUPS - 1)

    far = [(dz, dy) for d in range(5, 0, -1) for dz, dy in FAR if min(dz, 8 - dz) + dy == d]
    for k, (dz, dy) in enumerate(far):
        p = lax.rem(z + dz, 8) * 2 + lax.rem(y + dy, 2)
        col_out[k] = ready[tile(p), :].astype(BF16)
        pltpu.make_async_remote_copy(
            src_ref=col_out.at[k], dst_ref=col_in.at[k],
            send_sem=col_send, recv_sem=col_recv,
            device_id=(r, p), device_id_type=MESH).start()

    total = ready[tile(q), :]
    pltpu.make_async_copy(col_in, col_in, col_recv).wait()
    for k in range(COLS - 1):
        total += col_in[k].astype(F32)
    for a in range(2):
        halves = [total[:, a * 64 + i * 32:a * 64 + (i + 1) * 32] for i in range(2)]
        o_ref[a] = jnp.stack(halves, axis=1).astype(BF16)

    pltpu.make_async_copy(col_out, col_out, col_send).wait()

    @pl.loop(0, GROUPS)
    def _(g):
        core_copy(g).wait_send()
        pltpu.make_async_copy(row_in.at[g], row_in.at[g], row_send.at[g]).wait()
        pltpu.make_async_copy(wbuf.at[g * 2], wbuf.at[g * 2], w_send.at[g, 0]).wait()

        @pl.when(g != 6)
        def _():
            pltpu.make_async_copy(wbuf.at[g * 2 + 1], wbuf.at[g * 2 + 1], w_send.at[g, 1]).wait()


def shards(integrals, amplitudes):
    out = pl.pallas_call(
        kernel,
        out_shape=jax.ShapeDtypeStruct((2, VB, 2, OB), BF16),
        in_specs=[pl.BlockSpec(memory_space=pl.ANY)] * 2,
        out_specs=pl.BlockSpec(memory_space=pltpu.VMEM),
        scratch_shapes=[
            pltpu.VMEM((2 * GROUPS, CW, 2, DW * VB), BF16),
            pltpu.VMEM((CW, DW * PAIRS), BF16),
            pltpu.VMEM((PIECES, PAIRS, KP), BF16),
            pltpu.VMEM((KP, 128), BF16),
            pltpu.VMEM((GROUPS, SPAN, 128), F32),
            pltpu.VMEM((GROUPS, SPAN, 128), F32),
            pltpu.VMEM((GROUPS, CHIPS, 2, 64, 128), BF16),
            pltpu.VMEM((GROUPS, CHIPS - 1, 2, 64, 128), BF16),
            pltpu.VMEM((COLS, 32, 128), F32),
            pltpu.VMEM((SPAN, 128), F32),
            pltpu.VMEM((COLS * VB + VB, 128), F32),
            pltpu.VMEM((128 + 2, 128), F32),
            pltpu.VMEM((COLS - 1, 32, 128), BF16),
            pltpu.VMEM((COLS - 1, 32, 128), BF16),
            pltpu.SemaphoreType.DMA((GROUPS, 2)),
            pltpu.SemaphoreType.DMA((GROUPS, 2, PIECES)),
            pltpu.SemaphoreType.DMA,
            pltpu.SemaphoreType.DMA((GROUPS,)),
            pltpu.SemaphoreType.DMA((GROUPS,)),
            pltpu.SemaphoreType.DMA((GROUPS,)),
            pltpu.SemaphoreType.DMA((GROUPS,)),
            pltpu.SemaphoreType.DMA,
            pltpu.SemaphoreType.DMA,
        ],
        compiler_params=pltpu.CompilerParams(
            collective_id=0, has_side_effects=True, vmem_limit_bytes=56 * 2**20),
        cost_estimate=pl.CostEstimate(flops=13 * 10**9, bytes_accessed=13 * 10**6, transcendentals=0),
    )(integrals, amplitudes)
    return out


def solution(mesh):
    return jax.shard_map(
        shards,
        mesh=mesh,
        in_specs=(P("row", "col", None), P("row", "col")),
        out_specs=P("col", None, "row", None),
        check_vma=False,
    )
```
